1024 devices in a mesh: blk: 256 (over y_lo, z, x), rep: 4 (over y_hi, core).
Axes of the slice: x: 4, y: 4 (y_hi: 2, y_lo: 2; y = y_hi * 2 + y_lo), z: 32, core: 2. Of those that a mesh axis runs over, the one named last changes fastest.
Arguments:
- images: bfloat16 [131072, 1152], P(('blk', 'rep')), may hold values from -0.5 to 0.5
- texts: bfloat16 [131072, 1152], P('blk'), may hold values from -0.5 to 0.5
- positive: int32 [131072], P(('blk', 'rep')), may hold values from 0 to 131071, as said below
- temp_log: float32 [1], replicated, may hold values from 2 to 2.7
- bias_arg: float32 [1], replicated, may hold values from -5 to -2.5
Outputs:
- loss: float32 [1], replicated
- image_grad: float32 [131072, 1152], P(('blk', 'rep'))
- text_grad: float32 [131072, 1152], P(('blk', 'rep'))
- temp_grad: float32 [1], replicated
- bias_grad: float32 [1], replicated
The draws below stay inside these ranges and needn't reach their ends.
Inputs may be any that keep to these rules, and one draw needn't show every extreme that they name: `positive`: positive_i lies in a text shard whose index differs from i // 512 by at most 2 around the cycle of 256 shards.
All inputs are finite; a program needn't handle non-finite values.
Results may differ from the reference program's by a relative error of at most 0.0009.
Values may be sent and summed in bfloat16 or wider, within the bound.
No kernel may reach another device: no remote copies, remote signals or barrier semaphores. Data moves between devices by JAX's collectives and lax.ppermute only.
A program may use at most 32 MiB of HBM per device.

```python
import jax
import jax.numpy as jnp
from jax import lax

D = 1152
HALF = 2
TXT_SHARD = 512
BATCH = 131072


def pairing(key):
    key = jax.random.fold_in(key, 101)
    leading_shard, second, third = jax.random.split(key, 3)
    shards = BATCH // TXT_SHARD
    index = jnp.arange(BATCH, dtype=jnp.int32)
    shard = index // TXT_SHARD
    offset = jax.random.randint(leading_shard, (BATCH,), -HALF, HALF + 1, dtype=jnp.int32)
    within = jax.random.randint(second, (BATCH,), 0, TXT_SHARD, dtype=jnp.int32)
    chosen = (shard + offset) % shards * TXT_SHARD + within
    chosen = jnp.where(index == 0, 0, chosen)
    chosen = jnp.where(index == BATCH - 1, BATCH - 1, chosen)
    groups = jax.random.randint(third, (BATCH,), 0, 16, dtype=jnp.int32)
    return (chosen.astype(jnp.int32), groups)


def anchors(key):
    key = jax.random.fold_in(key, 202)
    leading_shard, second = jax.random.split(key, 2)
    table = jax.random.normal(leading_shard, (16, D), jnp.float32)
    reach = jax.random.uniform(second, (16, 1), jnp.float32, 0.3, 0.65)
    return table * reach


def draw_positive(key, part):
    chosen, groups = pairing(key)
    return chosen


def draw_images(key, part):
    chosen, groups = pairing(key)
    table = anchors(key)
    key = jax.random.fold_in(key, 3)
    leading_shard = jax.random.fold_in(key, 0)
    centre = table[groups[chosen]]
    values = jax.random.normal(leading_shard, (BATCH, D), jnp.float32) + centre
    return jnp.clip(0.03 * values, -0.5, 0.5).astype(jnp.bfloat16)


def draw_texts(key, part):
    chosen, groups = pairing(key)
    table = anchors(key)
    key = jax.random.fold_in(key, 5)
    leading_shard = jax.random.fold_in(key, 0)
    centre = table[groups]
    values = jax.random.normal(leading_shard, (BATCH, D), jnp.float32) + centre
    return jnp.clip(0.03 * values, -0.5, 0.5).astype(jnp.bfloat16)


def setup_inputs(seed: int = 0) -> dict:
    seeds = jax.random.split(jax.random.key(seed), 6)
    return {
        "images": draw_images(jax.random.fold_in(seeds[5], 71), 0),
        "texts": draw_texts(jax.random.fold_in(seeds[5], 71), 0),
        "positive": draw_positive(jax.random.fold_in(seeds[5], 71), 0),
        "temp_log": jnp.clip(jax.random.uniform(seeds[3], (1,), jnp.float32, 2.0, 2.7), 2.0, 2.7),
        "bias_arg": jnp.clip(jax.random.uniform(seeds[4], (1,), jnp.float32, -5.0, -2.5), -5.0, -2.5),
    }


EPS = 1e-06

def normalize(values):
    full = values.astype(jnp.float32)
    factor = lax.rsqrt(lax.optimization_barrier(jnp.sum(full * full, axis=-1, keepdims=True)) + EPS)
    return (full * factor, factor)

def back_normal(unit_f, factor, dunit):
    return factor * (dunit - unit_f * lax.optimization_barrier(jnp.sum(unit_f * dunit, axis=-1, keepdims=True)))

def block_terms(image_unit, text_unit, positive_rows, leading_shard, logit_scale, logit_bias):
    similarity = jnp.dot(image_unit, text_unit.T, preferred_element_type=jnp.float32)
    logit = logit_scale * similarity + logit_bias
    cols = leading_shard + jnp.arange(text_unit.shape[0], dtype=jnp.int32)
    sign = jnp.where(positive_rows[:, None] == cols[None, :], 1.0, -1.0).astype(jnp.float32)
    summed = jnp.sum(jax.nn.softplus(-sign * logit))
    grads = -sign * jax.nn.sigmoid(-sign * logit)
    global_batch = grads.astype(jnp.bfloat16)
    dx = jnp.dot(global_batch, text_unit, preferred_element_type=jnp.float32)
    text_grad_rows = jnp.dot(global_batch.T, image_unit, preferred_element_type=jnp.float32)
    return (summed, jnp.sum(grads), jnp.sum(grads * similarity), dx, text_grad_rows)

def reference(images, texts, positive, temp_log, bias_arg):
    shards = BATCH // TXT_SHARD
    logit_scale = jnp.exp(temp_log[0])
    logit_bias = bias_arg[0]
    image_float, xfac = normalize(images)
    yf, yfac = normalize(texts)
    xs = image_float.astype(jnp.bfloat16).reshape(shards, TXT_SHARD, D)
    ys = yf.astype(jnp.bfloat16).reshape(shards, TXT_SHARD, D)
    ps = positive.reshape(shards, TXT_SHARD)

    def step(carry, shard):
        dy_all, summed, gsum, tsum = carry
        xblock = lax.dynamic_index_in_dim(xs, shard, 0, keepdims=False)
        pblock = lax.dynamic_index_in_dim(ps, shard, 0, keepdims=False)
        dx = jnp.zeros((TXT_SHARD, D), jnp.float32)
        for offset in range(-HALF, HALF + 1):
            other = ((shard + offset) % shards).astype(jnp.int32)
            yblock = lax.dynamic_index_in_dim(ys, other, 0, keepdims=False)
            loss_part, g_part, t_part, dx_part, dy_part = block_terms(xblock, yblock, pblock, other * TXT_SHARD, logit_scale, logit_bias)
            summed = summed + loss_part
            gsum = gsum + g_part
            tsum = tsum + t_part
            dx = dx + dx_part
            dy_all = dy_all.at[other].add(dy_part)
        return ((dy_all, summed, gsum, tsum), dx)
    zero = jnp.zeros((), jnp.float32)
    start = (jnp.zeros((shards, TXT_SHARD, D), jnp.float32), zero, zero, zero)
    (dy_all, summed, gsum, tsum), dx_all = lax.scan(step, start, jnp.arange(shards, dtype=jnp.int32))
    image_grad = back_normal(image_float, xfac, logit_scale * dx_all.reshape(BATCH, D))
    text_grad = back_normal(yf, yfac, logit_scale * dy_all.reshape(BATCH, D))
    loss = (summed / BATCH).reshape(1)
    return (loss, image_grad, text_grad, (logit_scale * tsum).reshape(1), gsum.reshape(1))
```

```python
import jax
import jax.numpy as jnp
from jax import lax
from jax.experimental import pallas as pl
from jax.experimental.pallas import tpu as pltpu
from jax.sharding import Mesh, PartitionSpec as P

EPS = 1e-06
BLK = ("y_lo", "z", "x")
PLANE = ("y_lo", "x", "y_hi", "core")
SIZES = (2, 32, 4, 2, 2)
WIDTH = 1152
IMAGES = 128
TEXTS = 512
PAD_ROWS = 16
PACKED = IMAGES + PAD_ROWS
BATCH = 131072
RING = 32
F32 = jnp.float32
BF16 = jnp.bfloat16


def shape(*dims, dtype=F32):
    return jax.ShapeDtypeStruct(dims, dtype)


def call(body, outs, *args, flops=0, smem_in=(), smem_out=()):
    moved = sum(a.size * a.dtype.itemsize for a in args)
    moved += sum(o.size * o.dtype.itemsize for o in outs)
    scalar = pl.BlockSpec(memory_space=pltpu.SMEM)
    vector = pl.BlockSpec(memory_space=pltpu.VMEM)
    return pl.pallas_call(
        body,
        out_shape=outs,
        in_specs=[scalar if k in smem_in else vector for k in range(len(args))],
        out_specs=[scalar if k in smem_out else vector for k in range(len(outs))],
        compiler_params=pltpu.CompilerParams(vmem_limit_bytes=20 * 1024 * 1024),
        cost_estimate=pl.CostEstimate(flops=flops, bytes_accessed=moved, transcendentals=0),
    )(*args)


def shifted(value, by):
    count = lax.axis_size(BLK)
    return lax.ppermute(value, BLK, [(i, (i + by) % count) for i in range(count)])


def swapped(value, axis):
    return lax.ppermute(value, axis, [(0, 1), (1, 0)])


def normalized(values):
    full = values.astype(F32)
    factor = lax.rsqrt(jnp.sum(full * full, axis=-1, keepdims=True) + EPS)
    return full * factor, factor


def back_normal(unit_f, factor, dunit):
    return factor * (dunit - unit_f * jnp.sum(unit_f * dunit, axis=-1, keepdims=True))


def pack_kernel(images_ref, positive_ref, out_ref):
    unit, _ = normalized(images_ref[...])
    out_ref[:IMAGES, :] = unit.astype(BF16)
    pos = positive_ref[...]
    row = lax.broadcasted_iota(jnp.int32, (PAD_ROWS, IMAGES), 0)
    digit = jnp.where(row == 0, pos >> 12, jnp.where(row == 1, (pos >> 6) & 63, pos & 63))
    out_ref[IMAGES:, :] = jnp.zeros((PAD_ROWS, WIDTH), BF16)
    out_ref[IMAGES:, :IMAGES] = digit.astype(F32).astype(BF16)


def pair_block(packed_ref, text_unit, place_ref, temp_ref, bias_ref):
    unit = packed_ref[:IMAGES, :]
    digits = packed_ref[IMAGES:, :IMAGES].astype(F32).astype(jnp.int32)
    row = lax.broadcasted_iota(jnp.int32, (PAD_ROWS, IMAGES), 0)
    weight = jnp.where(row == 0, 4096, jnp.where(row == 1, 64, jnp.where(row == 2, 1, 0)))
    pos = jnp.sum(digits * weight, axis=0, keepdims=True) - place_ref[0]
    sim = lax.dot_general(text_unit, unit, (((1,), (1,)), ((), ())), preferred_element_type=F32)
    scale = jnp.exp(jnp.full((1, IMAGES), temp_ref[0], F32))
    logit = scale * sim + bias_ref[0]
    matching = lax.broadcasted_iota(jnp.int32, (TEXTS, IMAGES), 0) == pos
    against = jnp.where(matching, -logit, logit)
    small = jnp.exp(-jnp.abs(against))
    soft = jnp.maximum(against, 0.0) + jnp.log1p(small)
    sigmoid = jnp.where(against >= 0, 1.0, small) / (1.0 + small)
    grads = jnp.where(matching, -sigmoid, sigmoid)
    rounded = grads.astype(BF16)
    image_part = lax.dot_general(rounded, text_unit, (((0,), (0,)), ((), ())), preferred_element_type=F32)
    sums = [jnp.sum(v, axis=0, keepdims=True) for v in (soft, grads, grads * sim)]
    return image_part, rounded, sums


def sums_tile(sums):
    return jnp.concatenate(sums + [jnp.zeros((5, IMAGES), F32)], axis=0)


def own_kernel(texts_ref, packed_ref, place_ref, temp_ref, bias_ref, text_ref, dx_ref, grads_ref, sums_ref):
    unit, _ = normalized(texts_ref[...])
    text_ref[...] = unit.astype(BF16)
    dx_ref[...], grads_ref[...], sums = pair_block(packed_ref, text_ref[...], place_ref, temp_ref, bias_ref)
    sums_ref[...] = sums_tile(sums)


def near_kernel(text_ref, left_ref, right_ref, place_ref, temp_ref, bias_ref, dxl_ref, dxr_ref, grads_ref, sums_ref):
    text_unit = text_ref[...]
    dxl_ref[...], grads_ref[:, :IMAGES], first = pair_block(left_ref, text_unit, place_ref, temp_ref, bias_ref)
    dxr_ref[...], grads_ref[:, IMAGES:], second = pair_block(right_ref, text_unit, place_ref, temp_ref, bias_ref)
    sums_ref[...] = sums_tile([a + b for a, b in zip(first, second)])


def far_kernel(text_ref, left_ref, right_ref, place_ref, temp_ref, bias_ref, own_ref, near_ref,
               dxl_ref, dxr_ref, grads_ref, row_ref):
    text_unit = text_ref[...]
    dxl_ref[...], grads_ref[:, :IMAGES], first = pair_block(left_ref, text_unit, place_ref, temp_ref, bias_ref)
    dxr_ref[...], grads_ref[:, IMAGES:], second = pair_block(right_ref, text_unit, place_ref, temp_ref, bias_ref)
    tile = sums_tile([a + b for a, b in zip(first, second)]) + own_ref[...] + near_ref[...]
    totals = jnp.sum(tile, axis=1, keepdims=True)
    lane = lax.broadcasted_iota(jnp.int32, (1, IMAGES), 1)
    row = sum(jnp.where(lane == k, totals[k:k + 1], 0.0) for k in range(3))
    row_ref[...] = jnp.broadcast_to(row[None], (RING, 1, IMAGES))


def text_part_kernel(place_ref, g0, g1, g2, x0, x1l, x1r, x2l, x2r, send_ref, keep_ref):
    core = place_ref[2]
    blocks = ((g0, 0, x0), (g1, 0, x1l), (g1, 1, x1r), (g2, 0, x2l), (g2, 1, x2r))
    for out_ref, owner in ((send_ref, 1 - core), (keep_ref, core)):
        for half in range(2):
            first = pl.multiple_of((2 * half + owner) * IMAGES, IMAGES)
            total = None
            for grads, k, unit in blocks:
                part = jnp.dot(
                    grads[pl.ds(first, IMAGES), k * IMAGES:(k + 1) * IMAGES],
                    unit[:IMAGES, :],
                    preferred_element_type=F32,
                )
                total = part if total is None else total + part
            out_ref[half] = total


def halve_kernel(place_ref, keep_ref, got_ref, send_ref, rest_ref):
    mine = place_ref[1]
    send_ref[...] = keep_ref[1 - mine] + got_ref[1 - mine]
    rest_ref[...] = keep_ref[mine] + got_ref[mine]


def text_end_kernel(place_ref, temp_ref, texts_ref, rest_ref, got_ref, out_ref):
    first = pl.multiple_of((2 * place_ref[1] + place_ref[2]) * IMAGES, IMAGES)
    unit, factor = normalized(texts_ref[pl.ds(first, IMAGES), :])
    scale = jnp.exp(jnp.full((1, WIDTH), temp_ref[0], F32))
    out_ref[...] = back_normal(unit, factor, scale * (rest_ref[...] + got_ref[...]))


def image_end_kernel(temp_ref, images_ref, d0, d1, d2, d3, d4, out_ref):
    unit, factor = normalized(images_ref[...])
    scale = jnp.exp(jnp.full((1, WIDTH), temp_ref[0], F32))
    total = (d0[...] + d1[...] + d2[...]) + (d3[...] + d4[...])
    out_ref[...] = back_normal(unit, factor, scale * total)


def again_kernel(row_ref, out_ref):
    total = jnp.sum(row_ref[...], axis=0, keepdims=True)
    out_ref[...] = jnp.broadcast_to(total, out_ref.shape)


def sums_end_kernel(temp_ref, row_ref, loss_ref, temp_grad_ref, bias_grad_ref):
    total = jnp.sum(row_ref[...], axis=0)
    lane = lax.broadcasted_iota(jnp.int32, (1, IMAGES), 1)
    scale = jnp.exp(jnp.full((1, IMAGES), temp_ref[0], F32))
    loss_ref[0] = jnp.sum(jnp.where(lane == 0, total, 0.0)) * (1.0 / BATCH)
    bias_grad_ref[0] = jnp.sum(jnp.where(lane == 1, total, 0.0))
    temp_grad_ref[0] = jnp.sum(jnp.where(lane == 2, total * scale, 0.0))


def per_device(images, texts, positive, temp_log, bias_arg):
    place = jnp.stack([lax.axis_index(BLK) * TEXTS, lax.axis_index("y_hi"), lax.axis_index("core")]).astype(jnp.int32)
    block_flops = 4 * TEXTS * IMAGES * WIDTH
    (mine,) = call(pack_kernel, [shape(PACKED, WIDTH, dtype=BF16)], images, positive.reshape(1, IMAGES))
    left = shifted(mine, 1)
    right = shifted(mine, -1)
    text_unit, dx0, g0, sums0 = call(
        own_kernel,
        [shape(TEXTS, WIDTH, dtype=BF16), shape(IMAGES, WIDTH), shape(TEXTS, IMAGES, dtype=BF16), shape(8, IMAGES)],
        texts, mine, place, temp_log, bias_arg, flops=block_flops, smem_in=(2, 3, 4),
    )
    left, right, text_unit = lax.optimization_barrier((left, right, text_unit))
    left2 = shifted(left, 1)
    right2 = shifted(right, -1)
    pair_outs = [shape(IMAGES, WIDTH), shape(IMAGES, WIDTH), shape(TEXTS, 2 * IMAGES, dtype=BF16)]
    dxl, dxr, g1, sums1 = call(
        near_kernel, pair_outs + [shape(8, IMAGES)],
        text_unit, left, right, place, temp_log, bias_arg, flops=2 * block_flops, smem_in=(3, 4, 5),
    )
    dxl2, dxr2, g2, row = call(
        far_kernel, pair_outs + [shape(RING, 1, IMAGES)],
        text_unit, left2, right2, place, temp_log, bias_arg, sums0, sums1,
        flops=2 * block_flops, smem_in=(3, 4, 5),
    )
    parts = [shifted(dxl, -1), shifted(dxr, 1), shifted(dxl2, -2), shifted(dxr2, 2)]
    row = lax.all_to_all(row, PLANE, 0, 0, tiled=True)
    send, keep = call(
        text_part_kernel, [shape(2, IMAGES, WIDTH), shape(2, IMAGES, WIDTH)],
        place, g0, g1, g2, mine, left, right, left2, right2, flops=10 * TEXTS * IMAGES * WIDTH, smem_in=(0,),
    )
    got = swapped(send, "core")
    (row,) = call(again_kernel, [shape(RING, 1, IMAGES)], row)
    row, got = lax.optimization_barrier((row, got))
    row = lax.all_to_all(row, "z", 0, 0, tiled=True)
    send, rest = call(halve_kernel, [shape(IMAGES, WIDTH)] * 2, place, keep, got, smem_in=(0,))
    got = swapped(send, "y_hi")
    (text_grad,) = call(
        text_end_kernel, [shape(IMAGES, WIDTH)], place, temp_log, texts, rest, got, smem_in=(0, 1)
    )
    (image_grad,) = call(
        image_end_kernel, [shape(IMAGES, WIDTH)], temp_log, images, dx0, *parts, smem_in=(0,)
    )
    row, image_grad, text_grad = lax.optimization_barrier((row, image_grad, text_grad))
    loss, temp_grad, bias_grad = call(
        sums_end_kernel, [shape(1)] * 3, temp_log, row, smem_in=(0,), smem_out=(0, 1, 2)
    )
    return (loss, image_grad, text_grad, temp_grad, bias_grad)


def solution(mesh):
    axes = BLK + ("y_hi", "core")
    fine = Mesh(mesh.devices.reshape(SIZES), axes)
    placed = (P(axes, None), P(BLK, None), P(axes), P(), P())
    return jax.shard_map(
        per_device,
        mesh=fine,
        in_specs=placed,
        out_specs=(P(), P(axes, None), P(axes, None), P(), P()),
        check_vma=False,
    )
```

```python
import jax
import jax.numpy as jnp
from jax import lax
from jax.experimental import pallas as pl
from jax.experimental.pallas import tpu as pltpu
from jax.sharding import Mesh, PartitionSpec as P

EPS = 1e-06
BLK = ("y_lo", "z", "x")
PLANE = ("y_lo", "x", "y_hi", "core")
SIZES = (2, 32, 4, 2, 2)
WIDTH = 1152
IMAGES = 128
TEXTS = 512
PAD_ROWS = 16
PACKED = IMAGES + PAD_ROWS
BATCH = 131072
RING = 32
F32 = jnp.float32
BF16 = jnp.bfloat16


def shape(*dims, dtype=F32):
    return jax.ShapeDtypeStruct(dims, dtype)


def call(body, outs, *args, flops=0, smem_in=(), smem_out=(), any_out=(), scratch=()):
    moved = sum(a.size * a.dtype.itemsize for a in args)
    moved += sum(o.size * o.dtype.itemsize for o in outs)
    scalar = pl.BlockSpec(memory_space=pltpu.SMEM)
    vector = pl.BlockSpec(memory_space=pltpu.VMEM)
    placed = pl.BlockSpec(memory_space=pl.ANY)
    return pl.pallas_call(
        body,
        out_shape=outs,
        in_specs=[scalar if k in smem_in else vector for k in range(len(args))],
        out_specs=[scalar if k in smem_out else placed if k in any_out else vector for k in range(len(outs))],
        scratch_shapes=list(scratch),
        compiler_params=pltpu.CompilerParams(vmem_limit_bytes=20 * 1024 * 1024),
        cost_estimate=pl.CostEstimate(flops=flops, bytes_accessed=moved, transcendentals=0),
    )(*args)


def to_side(value, by):
    count = lax.axis_size(BLK)
    pairs = []
    for shard in range(count):
        pairs.append((2 * shard, 2 * ((shard + by) % count)))
        pairs.append((2 * shard + 1, 2 * ((shard - by) % count) + 1))
    return lax.ppermute(value, BLK + ("core",), pairs)


def swapped(value, axis):
    return lax.ppermute(value, axis, [(0, 1), (1, 0)])


def normalized(values):
    full = values.astype(F32)
    factor = lax.rsqrt(jnp.sum(full * full, axis=-1, keepdims=True) + EPS)
    return full * factor, factor


def back_normal(unit_f, factor, dunit):
    return factor * (dunit - unit_f * jnp.sum(unit_f * dunit, axis=-1, keepdims=True))


def pack_kernel(mine_ref, other_ref, my_positive_ref, other_positive_ref, out_ref):
    row = lax.broadcasted_iota(jnp.int32, (PAD_ROWS, IMAGES), 0)
    for k, (images_ref, positive_ref) in enumerate(((mine_ref, my_positive_ref), (other_ref, other_positive_ref))):
        unit, _ = normalized(images_ref[...])
        out_ref[k, :IMAGES, :] = unit.astype(BF16)
        pos = positive_ref[...]
        digit = jnp.where(row == 0, pos >> 12, jnp.where(row == 1, (pos >> 6) & 63, pos & 63))
        out_ref[k, IMAGES:, :] = jnp.zeros((PAD_ROWS, WIDTH), BF16)
        out_ref[k, IMAGES:, :IMAGES] = digit.astype(F32).astype(BF16)


def pair_block(packed_ref, k, text_unit, place_ref, temp_ref, bias_ref):
    unit = packed_ref[k, :IMAGES, :]
    digits = packed_ref[k, IMAGES:, :IMAGES].astype(F32).astype(jnp.int32)
    row = lax.broadcasted_iota(jnp.int32, (PAD_ROWS, IMAGES), 0)
    weight = jnp.where(row == 0, 4096, jnp.where(row == 1, 64, jnp.where(row == 2, 1, 0)))
    pos = jnp.sum(digits * weight, axis=0, keepdims=True) - place_ref[0]
    sim = lax.dot_general(text_unit, unit, (((1,), (1,)), ((), ())), preferred_element_type=F32)
    scale = jnp.exp(jnp.full((1, IMAGES), temp_ref[0], F32))
    logit = scale * sim + bias_ref[0]
    matching = lax.broadcasted_iota(jnp.int32, (TEXTS, IMAGES), 0) == pos
    against = jnp.where(matching, -logit, logit)
    small = jnp.exp(-jnp.abs(against))
    soft = jnp.maximum(against, 0.0) + jnp.log1p(small)
    sigmoid = jnp.where(against >= 0, 1.0, small) / (1.0 + small)
    grads = jnp.where(matching, -sigmoid, sigmoid)
    rounded = grads.astype(BF16)
    image_part = lax.dot_general(rounded, text_unit, (((0,), (0,)), ((), ())), preferred_element_type=F32)
    sums = [jnp.sum(v, axis=0, keepdims=True) for v in (soft, grads, grads * sim)]
    return image_part, rounded, sums


def text_part(grads, packed_ref, k):
    return jnp.dot(grads, packed_ref[k, :IMAGES, :], preferred_element_type=F32)


def sums_tile(sums):
    return jnp.concatenate(sums + [jnp.zeros((5, IMAGES), F32)], axis=0)


def own_kernel(texts_ref, packed_ref, place_ref, temp_ref, bias_ref, text_ref, dx_ref, dy_ref, sums_ref):
    unit, _ = normalized(texts_ref[...])
    text_ref[...] = unit.astype(BF16)
    dx_ref[...], grads, sums = pair_block(packed_ref, 0, text_ref[...], place_ref, temp_ref, bias_ref)
    dy_ref[...] = text_part(grads, packed_ref, 0)
    sums_ref[...] = sums_tile(sums)


def both_blocks(text_ref, packed_ref, place_ref, temp_ref, bias_ref, dx_ref, staged, sems):
    text_unit = text_ref[...]
    grads, sums, copies = [], [], []
    for k in range(2):
        staged[k], rounded, part = pair_block(packed_ref, k, text_unit, place_ref, temp_ref, bias_ref)
        copy = pltpu.make_async_copy(staged.at[k], dx_ref.at[k], sems.at[k])
        copy.start()
        grads.append(rounded)
        sums.append(part)
        copies.append(copy)
    return grads, sums_tile([a + b for a, b in zip(*sums)]), copies


def near_kernel(text_ref, packed_ref, place_ref, temp_ref, bias_ref, old_dy_ref, old_sums_ref,
                dx_ref, dy_ref, sums_ref, staged, sems):
    grads, tile, copies = both_blocks(text_ref, packed_ref, place_ref, temp_ref, bias_ref, dx_ref, staged, sems)
    dy_ref[...] = old_dy_ref[...] + text_part(grads[0], packed_ref, 0) + text_part(grads[1], packed_ref, 1)
    sums_ref[...] = old_sums_ref[...] + tile
    for copy in copies:
        copy.wait()


def far_kernel(text_ref, packed_ref, place_ref, temp_ref, bias_ref, old_dy_ref, old_sums_ref,
               dx_ref, send_ref, keep_ref, row_ref, staged, sems, total):
    grads, tile, copies = both_blocks(text_ref, packed_ref, place_ref, temp_ref, bias_ref, dx_ref, staged, sems)
    total[...] = old_dy_ref[...] + text_part(grads[0], packed_ref, 0) + text_part(grads[1], packed_ref, 1)
    core = place_ref[2]
    for out_ref, owner in ((send_ref, 1 - core), (keep_ref, core)):
        for half in range(2):
            first = pl.multiple_of((2 * half + owner) * IMAGES, IMAGES)
            out_ref[half] = total[pl.ds(first, IMAGES), :]
    totals = jnp.sum(old_sums_ref[...] + tile, axis=1, keepdims=True)
    lane = lax.broadcasted_iota(jnp.int32, (1, IMAGES), 1)
    row = sum(jnp.where(lane == k, totals[k:k + 1], 0.0) for k in range(3))
    row_ref[...] = jnp.broadcast_to(row[None], row_ref.shape)
    for copy in copies:
        copy.wait()


def halve_kernel(place_ref, keep_ref, got_ref, send_ref, rest_ref):
    mine = place_ref[1]
    send_ref[...] = keep_ref[1 - mine] + got_ref[1 - mine]
    rest_ref[...] = keep_ref[mine] + got_ref[mine]


def prepare_kernel(place_ref, texts_ref, unit_ref, factor_ref):
    first = pl.multiple_of((2 * place_ref[1] + place_ref[2]) * IMAGES, IMAGES)
    unit_ref[...], factor = normalized(texts_ref[pl.ds(first, IMAGES), :])
    factor_ref[...] = jnp.broadcast_to(factor, factor_ref.shape)


def text_end_kernel(temp_ref, unit_ref, factor_ref, rest_ref, got_ref, out_ref):
    scale = jnp.exp(jnp.full((1, WIDTH), temp_ref[0], F32))
    out_ref[...] = back_normal(unit_ref[...], factor_ref[:, :1], scale * (rest_ref[...] + got_ref[...]))


def near_join_kernel(own_ref, near_ref, mine_ref):
    mine_ref[...] = own_ref[...] + near_ref[0]


def join_kernel(partial_ref, near_ref, far_ref, mine_ref, other_ref):
    mine_ref[...] = partial_ref[...] + far_ref[0]
    other_ref[...] = near_ref[1] + far_ref[1]


def image_end_kernel(temp_ref, images_ref, mine_ref, got_ref, out_ref):
    unit, factor = normalized(images_ref[...])
    scale = jnp.exp(jnp.full((1, WIDTH), temp_ref[0], F32))
    out_ref[...] = back_normal(unit, factor, scale * (mine_ref[...] + got_ref[...]))


def again_kernel(row_ref, out_ref):
    total = jnp.sum(row_ref[...], axis=0, keepdims=True)
    out_ref[...] = jnp.broadcast_to(total, out_ref.shape)


def sums_end_kernel(temp_ref, row_ref, loss_ref, temp_grad_ref, bias_grad_ref):
    total = jnp.sum(row_ref[...], axis=0)
    lane = lax.broadcasted_iota(jnp.int32, (1, IMAGES), 1)
    scale = jnp.exp(jnp.full((1, IMAGES), temp_ref[0], F32))
    loss_ref[0] = jnp.sum(jnp.where(lane == 0, total, 0.0)) * (1.0 / BATCH)
    bias_grad_ref[0] = jnp.sum(jnp.where(lane == 1, total, 0.0))
    temp_grad_ref[0] = jnp.sum(jnp.where(lane == 2, total * scale, 0.0))


def per_device(images, texts, positive, temp_log, bias_arg):
    place = jnp.stack([lax.axis_index(BLK) * TEXTS, lax.axis_index("y_hi"), lax.axis_index("core")]).astype(jnp.int32)
    block_flops = 6 * TEXTS * IMAGES * WIDTH
    positive = positive.reshape(1, IMAGES)
    (packed,) = call(
        pack_kernel, [shape(2, PACKED, WIDTH, dtype=BF16)],
        images, swapped(images, "core"), positive, swapped(positive, "core"),
    )
    near = to_side(packed, 1)
    text_unit, dx0, dy, sums = call(
        own_kernel,
        [shape(TEXTS, WIDTH, dtype=BF16), shape(IMAGES, WIDTH), shape(TEXTS, WIDTH), shape(8, IMAGES)],
        texts, packed, place, temp_log, bias_arg, flops=block_flops, smem_in=(2, 3, 4),
    )
    near, text_unit = lax.optimization_barrier((near, text_unit))
    far = to_side(near, 1)
    staging = [pltpu.VMEM((2, IMAGES, WIDTH), F32), pltpu.SemaphoreType.DMA((2,))]
    near_dx, dy, sums = call(
        near_kernel, [shape(2, IMAGES, WIDTH), shape(TEXTS, WIDTH), shape(8, IMAGES)],
        text_unit, near, place, temp_log, bias_arg, dy, sums,
        flops=2 * block_flops, smem_in=(2, 3, 4), any_out=(0,), scratch=staging,
    )
    near_dx = to_side(near_dx, -1)
    far_dx, send, keep, row = call(
        far_kernel, [shape(2, IMAGES, WIDTH)] * 3 + [shape(RING, 1, IMAGES)],
        text_unit, far, place, temp_log, bias_arg, dy, sums,
        flops=2 * block_flops, smem_in=(2, 3, 4), any_out=(0,),
        scratch=staging + [pltpu.VMEM((TEXTS, WIDTH), F32)],
    )
    far_dx = to_side(far_dx, -2)
    got = swapped(send, "core")
    row = lax.all_to_all(row, "z", 0, 0, tiled=True)
    (mine,) = call(near_join_kernel, [shape(IMAGES, WIDTH)], dx0, near_dx, flops=2 * 10**9)
    mine, got = lax.optimization_barrier((mine, got))
    send, rest = call(halve_kernel, [shape(IMAGES, WIDTH)] * 2, place, keep, got, smem_in=(0,))
    got = swapped(send, "y_hi")
    unit, factor = call(
        prepare_kernel, [shape(IMAGES, WIDTH), shape(IMAGES, IMAGES)], place, texts, smem_in=(0,)
    )
    row, unit = lax.optimization_barrier((row, unit))
    (row,) = call(again_kernel, [shape(RING, 1, IMAGES)], row, flops=6 * 10**9)
    row = lax.all_to_all(row, PLANE, 0, 0, tiled=True)
    mine, other = call(join_kernel, [shape(IMAGES, WIDTH)] * 2, mine, near_dx, far_dx)
    other = swapped(other, "core")
    (text_grad,) = call(
        text_end_kernel, [shape(IMAGES, WIDTH)], temp_log, unit, factor, rest, got,
        smem_in=(0,),
    )
    mine, text_grad = lax.optimization_barrier((mine, text_grad))
    (image_grad,) = call(
        image_end_kernel, [shape(IMAGES, WIDTH)], temp_log, images, mine, other, smem_in=(0,)
    )
    row, image_grad, text_grad = lax.optimization_barrier((row, image_grad, text_grad))
    loss, temp_grad, bias_grad = call(
        sums_end_kernel, [shape(1)] * 3, temp_log, row, smem_in=(0,), smem_out=(0, 1, 2)
    )
    return (loss, image_grad, text_grad, temp_grad, bias_grad)


def solution(mesh):
    axes = BLK + ("y_hi", "core")
    fine = Mesh(mesh.devices.reshape(SIZES), axes)
    placed = (P(axes, None), P(BLK, None), P(axes), P(), P())
    return jax.shard_map(
        per_device,
        mesh=fine,
        in_specs=placed,
        out_specs=(P(), P(axes, None), P(axes, None), P(), P()),
        check_vma=False,
    )
```

```python
import jax
import jax.numpy as jnp
from jax import lax
from jax.experimental import pallas as pl
from jax.experimental.pallas import tpu as pltpu
from jax.sharding import Mesh, PartitionSpec as P

EPS = 1e-06
BLK = ("y_lo", "z", "x")
PLANE = ("y_lo", "x", "y_hi", "core")
SIZES = (2, 32, 4, 2, 2)
WIDTH = 1152
IMAGES = 128
TEXTS = 512
PAD_ROWS = 16
PAIR = 2 * IMAGES
BATCH = 131072
RING = 32
F32 = jnp.float32
BF16 = jnp.bfloat16


def shape(*dims, dtype=F32):
    return jax.ShapeDtypeStruct(dims, dtype)


def call(body, outs, *args, flops=0, smem_in=(), smem_out=(), any_out=(), scratch=()):
    moved = sum(a.size * a.dtype.itemsize for a in args)
    moved += sum(o.size * o.dtype.itemsize for o in outs)
    scalar = pl.BlockSpec(memory_space=pltpu.SMEM)
    vector = pl.BlockSpec(memory_space=pltpu.VMEM)
    placed = pl.BlockSpec(memory_space=pl.ANY)
    return pl.pallas_call(
        body,
        out_shape=outs,
        in_specs=[scalar if k in smem_in else vector for k in range(len(args))],
        out_specs=[scalar if k in smem_out else placed if k in any_out else vector for k in range(len(outs))],
        scratch_shapes=list(scratch),
        compiler_params=pltpu.CompilerParams(vmem_limit_bytes=20 * 1024 * 1024),
        cost_estimate=pl.CostEstimate(flops=flops, bytes_accessed=moved, transcendentals=0),
    )(*args)


def to_side(value, by):
    count = lax.axis_size(BLK)
    pairs = []
    for shard in range(count):
        pairs.append((2 * shard, 2 * ((shard + by) % count)))
        pairs.append((2 * shard + 1, 2 * ((shard - by) % count) + 1))
    return lax.ppermute(value, BLK + ("core",), pairs)


def swapped(value, axis):
    return lax.ppermute(value, axis, [(0, 1), (1, 0)])


def normalized(values):
    full = values.astype(F32)
    factor = lax.rsqrt(jnp.sum(full * full, axis=-1, keepdims=True) + EPS)
    return full * factor, factor


def back_normal(unit_f, factor, dunit):
    return factor * (dunit - unit_f * jnp.sum(unit_f * dunit, axis=-1, keepdims=True))


def pack_kernel(images_ref, positive_ref, out_ref):
    unit, _ = normalized(images_ref[...])
    out_ref[:IMAGES, :] = unit.astype(BF16)
    pos = positive_ref[...]
    row = lax.broadcasted_iota(jnp.int32, (PAD_ROWS, IMAGES), 0)
    digit = jnp.where(row == 0, pos >> 12, jnp.where(row == 1, (pos >> 6) & 63, pos & 63))
    out_ref[IMAGES:, :] = jnp.zeros((PAD_ROWS, WIDTH), BF16)
    out_ref[IMAGES:, :IMAGES] = digit.astype(F32).astype(BF16)


def stack_kernel(mine_ref, other_ref, out_ref):
    out_ref[:IMAGES, :] = mine_ref[:IMAGES, :]
    out_ref[IMAGES:PAIR, :] = other_ref[:IMAGES, :]
    out_ref[PAIR:, :] = mine_ref[IMAGES:, :]
    out_ref[PAIR:, IMAGES:PAIR] = other_ref[IMAGES:, :IMAGES]


def pair_block(packed_ref, text_unit, place_ref, temp_ref, bias_ref):
    count = packed_ref.shape[0] - PAD_ROWS
    unit = packed_ref[:count, :]
    digits = packed_ref[count:, :count].astype(F32).astype(jnp.int32)
    row = lax.broadcasted_iota(jnp.int32, (PAD_ROWS, count), 0)
    weight = jnp.where(row == 0, 4096, jnp.where(row == 1, 64, jnp.where(row == 2, 1, 0)))
    pos = jnp.sum(digits * weight, axis=0, keepdims=True) - place_ref[0]
    sim = lax.dot_general(text_unit, unit, (((1,), (1,)), ((), ())), preferred_element_type=F32)
    scale = jnp.exp(jnp.full((1, count), temp_ref[0], F32))
    logit = scale * sim + bias_ref[0]
    matching = lax.broadcasted_iota(jnp.int32, (TEXTS, count), 0) == pos
    against = jnp.where(matching, -logit, logit)
    small = jnp.exp(-jnp.abs(against))
    soft = jnp.maximum(against, 0.0) + jnp.log1p(small)
    sigmoid = jnp.where(against >= 0, 1.0, small) / (1.0 + small)
    grads = jnp.where(matching, -sigmoid, sigmoid)
    sums = [jnp.sum(v, axis=0, keepdims=True) for v in (soft, grads, grads * sim)]
    tile = jnp.concatenate(sums + [jnp.zeros((5, count), F32)], axis=0)
    for first in range(IMAGES, count, IMAGES):
        tile = tile[:, :IMAGES] + tile[:, first:first + IMAGES]
    return unit, grads.astype(BF16), tile


def image_part(grads, text_unit):
    return lax.dot_general(grads, text_unit, (((0,), (0,)), ((), ())), preferred_element_type=F32)


def text_part(grads, unit):
    return jnp.dot(grads, unit, preferred_element_type=F32)


def own_kernel(texts_ref, packed_ref, place_ref, temp_ref, bias_ref, text_ref, dx_ref, dy_ref, sums_ref):
    unit, _ = normalized(texts_ref[...])
    text_ref[...] = unit.astype(BF16)
    text_unit = text_ref[...]
    unit, grads, sums_ref[...] = pair_block(packed_ref, text_unit, place_ref, temp_ref, bias_ref)
    dx_ref[...] = image_part(grads, text_unit)
    dy_ref[...] = text_part(grads, unit)


def near_kernel(text_ref, packed_ref, place_ref, temp_ref, bias_ref, old_dy_ref, old_sums_ref,
                dx_ref, dy_ref, sums_ref, staged, sem):
    text_unit = text_ref[...]
    unit, grads, tile = pair_block(packed_ref, text_unit, place_ref, temp_ref, bias_ref)
    staged[...] = image_part(grads, text_unit)
    copy = pltpu.make_async_copy(staged, dx_ref, sem)
    copy.start()
    dy_ref[...] = old_dy_ref[...] + text_part(grads, unit)
    sums_ref[...] = old_sums_ref[...] + tile
    copy.wait()


def far_kernel(text_ref, packed_ref, place_ref, temp_ref, bias_ref, old_dy_ref, old_sums_ref,
               dx_ref, send_ref, keep_ref, row_ref, staged, sem, total):
    text_unit = text_ref[...]
    unit, grads, tile = pair_block(packed_ref, text_unit, place_ref, temp_ref, bias_ref)
    staged[...] = image_part(grads, text_unit)
    copy = pltpu.make_async_copy(staged, dx_ref, sem)
    copy.start()
    total[...] = old_dy_ref[...] + text_part(grads, unit)
    core = place_ref[2]
    for out_ref, owner in ((send_ref, 1 - core), (keep_ref, core)):
        for half in range(2):
            first = pl.multiple_of((2 * half + owner) * IMAGES, IMAGES)
            out_ref[half] = total[pl.ds(first, IMAGES), :]
    totals = jnp.sum(old_sums_ref[...] + tile, axis=1, keepdims=True)
    lane = lax.broadcasted_iota(jnp.int32, (1, IMAGES), 1)
    row = sum(jnp.where(lane == k, totals[k:k + 1], 0.0) for k in range(3))
    row_ref[...] = jnp.broadcast_to(row[None], row_ref.shape)
    copy.wait()


def halve_kernel(place_ref, keep_ref, got_ref, send_ref, rest_ref):
    mine = place_ref[1]
    send_ref[...] = keep_ref[1 - mine] + got_ref[1 - mine]
    rest_ref[...] = keep_ref[mine] + got_ref[mine]


def prepare_kernel(place_ref, texts_ref, unit_ref, factor_ref):
    first = pl.multiple_of((2 * place_ref[1] + place_ref[2]) * IMAGES, IMAGES)
    unit_ref[...], factor = normalized(texts_ref[pl.ds(first, IMAGES), :])
    factor_ref[...] = jnp.broadcast_to(factor, factor_ref.shape)


def text_end_kernel(temp_ref, unit_ref, factor_ref, rest_ref, got_ref, out_ref):
    scale = jnp.exp(jnp.full((1, WIDTH), temp_ref[0], F32))
    out_ref[...] = back_normal(unit_ref[...], factor_ref[:, :1], scale * (rest_ref[...] + got_ref[...]))


def join_kernel(own_ref, near_ref, far_ref, mine_ref, other_ref):
    mine_ref[...] = own_ref[...] + near_ref[:IMAGES, :] + far_ref[:IMAGES, :]
    other_ref[...] = near_ref[IMAGES:, :] + far_ref[IMAGES:, :]


def image_end_kernel(temp_ref, images_ref, mine_ref, got_ref, out_ref):
    unit, factor = normalized(images_ref[...])
    scale = jnp.exp(jnp.full((1, WIDTH), temp_ref[0], F32))
    out_ref[...] = back_normal(unit, factor, scale * (mine_ref[...] + got_ref[...]))


def again_kernel(row_ref, out_ref):
    total = jnp.sum(row_ref[...], axis=0, keepdims=True)
    out_ref[...] = jnp.broadcast_to(total, out_ref.shape)


def sums_end_kernel(temp_ref, row_ref, loss_ref, temp_grad_ref, bias_grad_ref):
    total = jnp.sum(row_ref[...], axis=0)
    lane = lax.broadcasted_iota(jnp.int32, (1, IMAGES), 1)
    scale = jnp.exp(jnp.full((1, IMAGES), temp_ref[0], F32))
    loss_ref[0] = jnp.sum(jnp.where(lane == 0, total, 0.0)) * (1.0 / BATCH)
    bias_grad_ref[0] = jnp.sum(jnp.where(lane == 1, total, 0.0))
    temp_grad_ref[0] = jnp.sum(jnp.where(lane == 2, total * scale, 0.0))


def per_device(images, texts, positive, temp_log, bias_arg):
    place = jnp.stack([lax.axis_index(BLK) * TEXTS, lax.axis_index("y_hi"), lax.axis_index("core")]).astype(jnp.int32)
    block_flops = 6 * TEXTS * IMAGES * WIDTH
    positive = positive.reshape(1, IMAGES)
    (mine,) = call(pack_kernel, [shape(IMAGES + PAD_ROWS, WIDTH, dtype=BF16)], images, positive)
    (packed,) = call(stack_kernel, [shape(PAIR + PAD_ROWS, WIDTH, dtype=BF16)], mine, swapped(mine, "core"))
    near = to_side(packed, 1)
    text_unit, dx0, dy, sums = call(
        own_kernel,
        [shape(TEXTS, WIDTH, dtype=BF16), shape(IMAGES, WIDTH), shape(TEXTS, WIDTH), shape(8, IMAGES)],
        texts, mine, place, temp_log, bias_arg, flops=block_flops, smem_in=(2, 3, 4),
    )
    near, text_unit = lax.optimization_barrier((near, text_unit))
    far = to_side(near, 1)
    staging = [pltpu.VMEM((PAIR, WIDTH), F32), pltpu.SemaphoreType.DMA(())]
    near_dx, dy, sums = call(
        near_kernel, [shape(PAIR, WIDTH), shape(TEXTS, WIDTH), shape(8, IMAGES)],
        text_unit, near, place, temp_log, bias_arg, dy, sums,
        flops=2 * block_flops, smem_in=(2, 3, 4), any_out=(0,), scratch=staging,
    )
    near_dx = to_side(near_dx, -1)
    far_dx, send, keep, row = call(
        far_kernel, [shape(PAIR, WIDTH)] + [shape(2, IMAGES, WIDTH)] * 2 + [shape(RING, 1, IMAGES)],
        text_unit, far, place, temp_log, bias_arg, dy, sums,
        flops=2 * block_flops, smem_in=(2, 3, 4), any_out=(0,),
        scratch=staging + [pltpu.VMEM((TEXTS, WIDTH), F32)],
    )
    far_dx = to_side(far_dx, -2)
    got = swapped(send, "core")
    row = lax.all_to_all(row, "z", 0, 0, tiled=True)
    near_dx, got = lax.optimization_barrier((near_dx, got))
    send, rest = call(halve_kernel, [shape(IMAGES, WIDTH)] * 2, place, keep, got, smem_in=(0,))
    got = swapped(send, "y_hi")
    unit, factor = call(
        prepare_kernel, [shape(IMAGES, WIDTH), shape(IMAGES, IMAGES)], place, texts, smem_in=(0,)
    )
    row, unit = lax.optimization_barrier((row, unit))
    (row,) = call(again_kernel, [shape(RING, 1, IMAGES)], row, flops=5 * 10**9)
    row = lax.all_to_all(row, PLANE, 0, 0, tiled=True)
    mine, other = call(join_kernel, [shape(IMAGES, WIDTH)] * 2, dx0, near_dx, far_dx)
    other = swapped(other, "core")
    (text_grad,) = call(
        text_end_kernel, [shape(IMAGES, WIDTH)], temp_log, unit, factor, rest, got,
        smem_in=(0,), flops=8 * 10**9,
    )
    mine, text_grad = lax.optimization_barrier((mine, text_grad))
    (image_grad,) = call(
        image_end_kernel, [shape(IMAGES, WIDTH)], temp_log, images, mine, other, smem_in=(0,)
    )
    row, image_grad, text_grad = lax.optimization_barrier((row, image_grad, text_grad))
    loss, temp_grad, bias_grad = call(
        sums_end_kernel, [shape(1)] * 3, temp_log, row, smem_in=(0,), smem_out=(0, 1, 2)
    )
    return (loss, image_grad, text_grad, temp_grad, bias_grad)


def solution(mesh):
    axes = BLK + ("y_hi", "core")
    fine = Mesh(mesh.devices.reshape(SIZES), axes)
    placed = (P(axes, None), P(BLK, None), P(axes), P(), P())
    return jax.shard_map(
        per_device,
        mesh=fine,
        in_specs=placed,
        out_specs=(P(), P(axes, None), P(axes, None), P(), P()),
        check_vma=False,
    )
```

```python
import jax
import jax.numpy as jnp
from jax import lax
from jax.experimental import pallas as pl
from jax.experimental.pallas import tpu as pltpu
from jax.sharding import Mesh, PartitionSpec as P

EPS = 1e-06
BLK = ("y_lo", "z", "x")
PLANE = ("y_lo", "x", "y_hi", "core")
SIZES = (2, 32, 4, 2, 2)
WIDTH = 1152
IMAGES = 128
TEXTS = 512
PAD_ROWS = 16
PAIR = 2 * IMAGES
BATCH = 131072
RING = 32
F32 = jnp.float32
BF16 = jnp.bfloat16


def shape(*dims, dtype=F32):
    return jax.ShapeDtypeStruct(dims, dtype)


def call(body, outs, *args, flops=0, smem_in=(), smem_out=(), any_out=(), scratch=()):
    moved = sum(a.size * a.dtype.itemsize for a in args)
    moved += sum(o.size * o.dtype.itemsize for o in outs)
    scalar = pl.BlockSpec(memory_space=pltpu.SMEM)
    vector = pl.BlockSpec(memory_space=pltpu.VMEM)
    placed = pl.BlockSpec(memory_space=pl.ANY)
    return pl.pallas_call(
        body,
        out_shape=outs,
        in_specs=[scalar if k in smem_in else vector for k in range(len(args))],
        out_specs=[scalar if k in smem_out else placed if k in any_out else vector for k in range(len(outs))],
        scratch_shapes=list(scratch),
        compiler_params=pltpu.CompilerParams(vmem_limit_bytes=20 * 1024 * 1024),
        cost_estimate=pl.CostEstimate(flops=flops, bytes_accessed=moved, transcendentals=0),
    )(*args)


def to_side(value, by):
    count = lax.axis_size(BLK)
    pairs = []
    for shard in range(count):
        pairs.append((2 * shard, 2 * ((shard + by) % count)))
        pairs.append((2 * shard + 1, 2 * ((shard - by) % count) + 1))
    return lax.ppermute(value, BLK + ("core",), pairs)


def swapped(value, axis):
    return lax.ppermute(value, axis, [(0, 1), (1, 0)])


def normalized(values):
    full = values.astype(F32)
    factor = lax.rsqrt(jnp.sum(full * full, axis=-1, keepdims=True) + EPS)
    return full * factor, factor


def back_normal(unit_f, factor, dunit):
    return factor * (dunit - unit_f * jnp.sum(unit_f * dunit, axis=-1, keepdims=True))


def pack_kernel(images_ref, positive_ref, out_ref):
    unit, _ = normalized(images_ref[...])
    out_ref[:IMAGES, :] = unit.astype(BF16)
    pos = positive_ref[...]
    row = lax.broadcasted_iota(jnp.int32, (PAD_ROWS, IMAGES), 0)
    digit = jnp.where(row == 0, pos >> 12, jnp.where(row == 1, (pos >> 6) & 63, pos & 63))
    out_ref[IMAGES:, :] = jnp.zeros((PAD_ROWS, WIDTH), BF16)
    out_ref[IMAGES:, :IMAGES] = digit.astype(F32).astype(BF16)


def pair_block(packed_refs, text_unit, place_ref, temp_ref, bias_ref):
    count = len(packed_refs) * IMAGES
    unit = jnp.concatenate([ref[:IMAGES, :] for ref in packed_refs], axis=0)
    digits = jnp.concatenate([ref[IMAGES:, :IMAGES] for ref in packed_refs], axis=1).astype(F32).astype(jnp.int32)
    row = lax.broadcasted_iota(jnp.int32, (PAD_ROWS, count), 0)
    weight = jnp.where(row == 0, 4096, jnp.where(row == 1, 64, jnp.where(row == 2, 1, 0)))
    pos = jnp.sum(digits * weight, axis=0, keepdims=True) - place_ref[0]
    sim = lax.dot_general(text_unit, unit, (((1,), (1,)), ((), ())), preferred_element_type=F32)
    scale = jnp.exp(jnp.full((1, count), temp_ref[0], F32))
    logit = scale * sim + bias_ref[0]
    matching = lax.broadcasted_iota(jnp.int32, (TEXTS, count), 0) == pos
    against = jnp.where(matching, -logit, logit)
    small = jnp.exp(-jnp.abs(against))
    soft = jnp.maximum(against, 0.0) + jnp.log1p(small)
    sigmoid = jnp.where(against >= 0, 1.0, small) / (1.0 + small)
    grads = jnp.where(matching, -sigmoid, sigmoid)
    sums = [jnp.sum(v, axis=0, keepdims=True) for v in (soft, grads, grads * sim)]
    tile = jnp.concatenate(sums + [jnp.zeros((5, count), F32)], axis=0)
    for first in range(IMAGES, count, IMAGES):
        tile = tile[:, :IMAGES] + tile[:, first:first + IMAGES]
    return unit, grads.astype(BF16), tile


def image_part(grads, text_unit):
    return lax.dot_general(grads, text_unit, (((0,), (0,)), ((), ())), preferred_element_type=F32)


def text_part(grads, unit):
    return jnp.dot(grads, unit, preferred_element_type=F32)


def own_kernel(texts_ref, packed_ref, place_ref, temp_ref, bias_ref, text_ref, dx_ref, dy_ref, sums_ref):
    unit, _ = normalized(texts_ref[...])
    text_ref[...] = unit.astype(BF16)
    text_unit = text_ref[...]
    unit, grads, sums_ref[...] = pair_block([packed_ref], text_unit, place_ref, temp_ref, bias_ref)
    dx_ref[...] = image_part(grads, text_unit)
    dy_ref[...] = text_part(grads, unit)


def near_kernel(text_ref, first_ref, second_ref, place_ref, temp_ref, bias_ref, old_dy_ref, old_sums_ref,
                dx_ref, dy_ref, sums_ref, staged, sem):
    text_unit = text_ref[...]
    unit, grads, tile = pair_block([first_ref, second_ref], text_unit, place_ref, temp_ref, bias_ref)
    staged[...] = image_part(grads, text_unit)
    copy = pltpu.make_async_copy(staged, dx_ref, sem)
    copy.start()
    dy_ref[...] = old_dy_ref[...] + text_part(grads, unit)
    sums_ref[...] = old_sums_ref[...] + tile
    copy.wait()


def far_kernel(text_ref, first_ref, second_ref, place_ref, temp_ref, bias_ref, old_dy_ref, old_sums_ref,
               dx_ref, send_ref, keep_ref, row_ref, staged, sem, total):
    text_unit = text_ref[...]
    unit, grads, tile = pair_block([first_ref, second_ref], text_unit, place_ref, temp_ref, bias_ref)
    staged[...] = image_part(grads, text_unit)
    copy = pltpu.make_async_copy(staged, dx_ref, sem)
    copy.start()
    total[...] = old_dy_ref[...] + text_part(grads, unit)
    core = place_ref[2]
    for out_ref, owner in ((send_ref, 1 - core), (keep_ref, core)):
        for half in range(2):
            first = pl.multiple_of((2 * half + owner) * IMAGES, IMAGES)
            out_ref[half] = total[pl.ds(first, IMAGES), :]
    totals = jnp.sum(old_sums_ref[...] + tile, axis=1, keepdims=True)
    lane = lax.broadcasted_iota(jnp.int32, (1, IMAGES), 1)
    row = sum(jnp.where(lane == k, totals[k:k + 1], 0.0) for k in range(3))
    row_ref[...] = jnp.broadcast_to(row[None], row_ref.shape)
    copy.wait()


def halve_kernel(place_ref, keep_ref, got_ref, send_ref, rest_ref):
    mine = place_ref[1]
    send_ref[...] = keep_ref[1 - mine] + got_ref[1 - mine]
    rest_ref[...] = keep_ref[mine] + got_ref[mine]


def prepare_kernel(place_ref, texts_ref, unit_ref, factor_ref):
    first = pl.multiple_of((2 * place_ref[1] + place_ref[2]) * IMAGES, IMAGES)
    unit_ref[...], factor = normalized(texts_ref[pl.ds(first, IMAGES), :])
    factor_ref[...] = jnp.broadcast_to(factor, factor_ref.shape)


def text_end_kernel(temp_ref, unit_ref, factor_ref, rest_ref, got_ref, out_ref):
    scale = jnp.exp(jnp.full((1, WIDTH), temp_ref[0], F32))
    out_ref[...] = back_normal(unit_ref[...], factor_ref[:, :1], scale * (rest_ref[...] + got_ref[...]))


def join_kernel(own_ref, near_ref, far_ref, mine_ref, other_ref):
    mine_ref[...] = own_ref[...] + near_ref[:IMAGES, :] + far_ref[:IMAGES, :]
    other_ref[...] = near_ref[IMAGES:, :] + far_ref[IMAGES:, :]


def image_end_kernel(temp_ref, images_ref, mine_ref, got_ref, out_ref):
    unit, factor = normalized(images_ref[...])
    scale = jnp.exp(jnp.full((1, WIDTH), temp_ref[0], F32))
    out_ref[...] = back_normal(unit, factor, scale * (mine_ref[...] + got_ref[...]))


def again_kernel(row_ref, out_ref):
    total = jnp.sum(row_ref[...], axis=0, keepdims=True)
    out_ref[...] = jnp.broadcast_to(total, out_ref.shape)


def sums_end_kernel(temp_ref, row_ref, loss_ref, temp_grad_ref, bias_grad_ref):
    total = jnp.sum(row_ref[...], axis=0)
    lane = lax.broadcasted_iota(jnp.int32, (1, IMAGES), 1)
    scale = jnp.exp(jnp.full((1, IMAGES), temp_ref[0], F32))
    loss_ref[0] = jnp.sum(jnp.where(lane == 0, total, 0.0)) * (1.0 / BATCH)
    bias_grad_ref[0] = jnp.sum(jnp.where(lane == 1, total, 0.0))
    temp_grad_ref[0] = jnp.sum(jnp.where(lane == 2, total * scale, 0.0))


def per_device(images, texts, positive, temp_log, bias_arg):
    place = jnp.stack([lax.axis_index(BLK) * TEXTS, lax.axis_index("y_hi"), lax.axis_index("core")]).astype(jnp.int32)
    block_flops = 6 * TEXTS * IMAGES * WIDTH
    positive = positive.reshape(1, IMAGES)
    (mine,) = call(pack_kernel, [shape(IMAGES + PAD_ROWS, WIDTH, dtype=BF16)], images, positive)
    other = swapped(mine, "core")
    near = [to_side(mine, 1), to_side(other, 1)]
    text_unit, dx0, dy, sums = call(
        own_kernel,
        [shape(TEXTS, WIDTH, dtype=BF16), shape(IMAGES, WIDTH), shape(TEXTS, WIDTH), shape(8, IMAGES)],
        texts, mine, place, temp_log, bias_arg, flops=block_flops, smem_in=(2, 3, 4),
    )
    near[0], text_unit = lax.optimization_barrier((near[0], text_unit))
    far = [to_side(near[0], 1), to_side(near[1], 1)]
    staging = [pltpu.VMEM((PAIR, WIDTH), F32), pltpu.SemaphoreType.DMA(())]
    near_dx, dy, sums = call(
        near_kernel, [shape(PAIR, WIDTH), shape(TEXTS, WIDTH), shape(8, IMAGES)],
        text_unit, *near, place, temp_log, bias_arg, dy, sums,
        flops=2 * block_flops, smem_in=(3, 4, 5), any_out=(0,), scratch=staging,
    )
    near_dx = to_side(near_dx, -1)
    far_dx, send, keep, row = call(
        far_kernel, [shape(PAIR, WIDTH)] + [shape(2, IMAGES, WIDTH)] * 2 + [shape(RING, 1, IMAGES)],
        text_unit, *far, place, temp_log, bias_arg, dy, sums,
        flops=2 * block_flops, smem_in=(3, 4, 5), any_out=(0,),
        scratch=staging + [pltpu.VMEM((TEXTS, WIDTH), F32)],
    )
    far_dx = to_side(far_dx, -2)
    got = swapped(send, "core")
    row = lax.all_to_all(row, "z", 0, 0, tiled=True)
    near_dx, got = lax.optimization_barrier((near_dx, got))
    send, rest = call(halve_kernel, [shape(IMAGES, WIDTH)] * 2, place, keep, got, smem_in=(0,))
    got = swapped(send, "y_hi")
    unit, factor = call(
        prepare_kernel, [shape(IMAGES, WIDTH), shape(IMAGES, IMAGES)], place, texts, smem_in=(0,)
    )
    row, unit = lax.optimization_barrier((row, unit))
    (row,) = call(again_kernel, [shape(RING, 1, IMAGES)], row, flops=5 * 10**9)
    row = lax.all_to_all(row, PLANE, 0, 0, tiled=True)
    mine, other = call(join_kernel, [shape(IMAGES, WIDTH)] * 2, dx0, near_dx, far_dx)
    other = swapped(other, "core")
    (text_grad,) = call(
        text_end_kernel, [shape(IMAGES, WIDTH)], temp_log, unit, factor, rest, got,
        smem_in=(0,), flops=8 * 10**9,
    )
    mine, text_grad = lax.optimization_barrier((mine, text_grad))
    (image_grad,) = call(
        image_end_kernel, [shape(IMAGES, WIDTH)], temp_log, images, mine, other, smem_in=(0,)
    )
    row, image_grad, text_grad = lax.optimization_barrier((row, image_grad, text_grad))
    loss, temp_grad, bias_grad = call(
        sums_end_kernel, [shape(1)] * 3, temp_log, row, smem_in=(0,), smem_out=(0, 1, 2)
    )
    return (loss, image_grad, text_grad, temp_grad, bias_grad)


def solution(mesh):
    axes = BLK + ("y_hi", "core")
    fine = Mesh(mesh.devices.reshape(SIZES), axes)
    placed = (P(axes, None), P(BLK, None), P(axes), P(), P())
    return jax.shard_map(
        per_device,
        mesh=fine,
        in_specs=placed,
        out_specs=(P(), P(axes, None), P(axes, None), P(), P()),
        check_vma=False,
    )
```

```python
import jax
import jax.numpy as jnp
from jax import lax
from jax.experimental import pallas as pl
from jax.experimental.pallas import tpu as pltpu
from jax.sharding import Mesh, PartitionSpec as P

EPS = 1e-06
BLK = ("y_lo", "z", "x")
PLANE = ("y_lo", "x", "y_hi", "core")
SIZES = (2, 32, 4, 2, 2)
WIDTH = 1152
IMAGES = 128
TEXTS = 512
PAD_ROWS = 16
PAIR = 2 * IMAGES
BATCH = 131072
RING = 32
F32 = jnp.float32
BF16 = jnp.bfloat16


def shape(*dims, dtype=F32):
    return jax.ShapeDtypeStruct(dims, dtype)


def call(body, outs, *args, flops=0, smem_in=(), smem_out=(), any_out=(), scratch=()):
    moved = sum(a.size * a.dtype.itemsize for a in args)
    moved += sum(o.size * o.dtype.itemsize for o in outs)
    scalar = pl.BlockSpec(memory_space=pltpu.SMEM)
    vector = pl.BlockSpec(memory_space=pltpu.VMEM)
    placed = pl.BlockSpec(memory_space=pl.ANY)
    return pl.pallas_call(
        body,
        out_shape=outs,
        in_specs=[scalar if k in smem_in else vector for k in range(len(args))],
        out_specs=[scalar if k in smem_out else placed if k in any_out else vector for k in range(len(outs))],
        scratch_shapes=list(scratch),
        compiler_params=pltpu.CompilerParams(vmem_limit_bytes=20 * 1024 * 1024),
        cost_estimate=pl.CostEstimate(flops=flops, bytes_accessed=moved, transcendentals=0),
    )(*args)


def to_side(value, by):
    count = lax.axis_size(BLK)
    pairs = []
    for shard in range(count):
        pairs.append((2 * shard, 2 * ((shard + by) % count)))
        pairs.append((2 * shard + 1, 2 * ((shard - by) % count) + 1))
    return lax.ppermute(value, BLK + ("core",), pairs)


def swapped(value, axis):
    return lax.ppermute(value, axis, [(0, 1), (1, 0)])


def normalized(values):
    full = values.astype(F32)
    factor = lax.rsqrt(jnp.sum(full * full, axis=-1, keepdims=True) + EPS)
    return full * factor, factor


def back_normal(unit_f, factor, dunit):
    return factor * (dunit - unit_f * jnp.sum(unit_f * dunit, axis=-1, keepdims=True))


def pack_kernel(images_ref, positive_ref, out_ref):
    unit, _ = normalized(images_ref[...])
    out_ref[:IMAGES, :] = unit.astype(BF16)
    pos = positive_ref[...]
    row = lax.broadcasted_iota(jnp.int32, (PAD_ROWS, IMAGES), 0)
    digit = jnp.where(row == 0, pos >> 12, jnp.where(row == 1, (pos >> 6) & 63, pos & 63))
    out_ref[IMAGES:, :] = jnp.zeros((PAD_ROWS, WIDTH), BF16)
    out_ref[IMAGES:, :IMAGES] = digit.astype(F32).astype(BF16)


def pair_block(packed_refs, text_unit, place_ref, temp_ref, bias_ref):
    count = len(packed_refs) * IMAGES
    unit = jnp.concatenate([ref[:IMAGES, :] for ref in packed_refs], axis=0)
    digits = jnp.concatenate([ref[IMAGES:, :IMAGES] for ref in packed_refs], axis=1).astype(F32).astype(jnp.int32)
    row = lax.broadcasted_iota(jnp.int32, (PAD_ROWS, count), 0)
    weight = jnp.where(row == 0, 4096, jnp.where(row == 1, 64, jnp.where(row == 2, 1, 0)))
    pos = jnp.sum(digits * weight, axis=0, keepdims=True) - place_ref[0]
    sim = lax.dot_general(text_unit, unit, (((1,), (1,)), ((), ())), preferred_element_type=F32)
    scale = jnp.exp(jnp.full((1, count), temp_ref[0], F32))
    logit = scale * sim + bias_ref[0]
    matching = lax.broadcasted_iota(jnp.int32, (TEXTS, count), 0) == pos
    against = jnp.where(matching, -logit, logit)
    small = jnp.exp(-jnp.abs(against))
    soft = jnp.maximum(against, 0.0) + jnp.log1p(small)
    sigmoid = jnp.where(against >= 0, 1.0, small) / (1.0 + small)
    grads = jnp.where(matching, -sigmoid, sigmoid)
    sums = [jnp.sum(v, axis=0, keepdims=True) for v in (soft, grads, grads * sim)]
    tile = jnp.concatenate(sums + [jnp.zeros((5, count), F32)], axis=0)
    for first in range(IMAGES, count, IMAGES):
        tile = tile[:, :IMAGES] + tile[:, first:first + IMAGES]
    return unit, grads.astype(BF16), tile


def image_part(grads, text_unit):
    return lax.dot_general(grads, text_unit, (((0,), (0,)), ((), ())), preferred_element_type=F32)


def text_part(grads, unit):
    return jnp.dot(grads, unit, preferred_element_type=F32)


def own_kernel(texts_ref, packed_ref, place_ref, temp_ref, bias_ref, text_ref, dx_ref, grads_ref, sums_ref):
    unit, _ = normalized(texts_ref[...])
    text_ref[...] = unit.astype(BF16)
    text_unit = text_ref[...]
    _, grads_ref[...], sums_ref[...] = pair_block([packed_ref], text_unit, place_ref, temp_ref, bias_ref)
    dx_ref[...] = image_part(grads_ref[...], text_unit)


def near_kernel(text_ref, first_ref, second_ref, place_ref, temp_ref, bias_ref, own_ref, own_grads_ref, old_sums_ref,
                dx_ref, dy_ref, sums_ref, staged, sem):
    text_unit = text_ref[...]
    unit, grads, tile = pair_block([first_ref, second_ref], text_unit, place_ref, temp_ref, bias_ref)
    staged[...] = image_part(grads, text_unit)
    copy = pltpu.make_async_copy(staged, dx_ref, sem)
    copy.start()
    dy_ref[...] = text_part(own_grads_ref[...], own_ref[:IMAGES, :]) + text_part(grads, unit)
    sums_ref[...] = old_sums_ref[...] + tile
    copy.wait()


def far_kernel(text_ref, first_ref, second_ref, place_ref, temp_ref, bias_ref, old_dy_ref, old_sums_ref,
               dx_ref, send_ref, keep_ref, row_ref, staged, sem, total):
    text_unit = text_ref[...]
    unit, grads, tile = pair_block([first_ref, second_ref], text_unit, place_ref, temp_ref, bias_ref)
    staged[...] = image_part(grads, text_unit)
    copy = pltpu.make_async_copy(staged, dx_ref, sem)
    copy.start()
    total[...] = old_dy_ref[...] + text_part(grads, unit)
    core = place_ref[2]
    for out_ref, owner in ((send_ref, 1 - core), (keep_ref, core)):
        for half in range(2):
            first = pl.multiple_of((2 * half + owner) * IMAGES, IMAGES)
            out_ref[half] = total[pl.ds(first, IMAGES), :]
    totals = jnp.sum(old_sums_ref[...] + tile, axis=1, keepdims=True)
    lane = lax.broadcasted_iota(jnp.int32, (1, IMAGES), 1)
    row = sum(jnp.where(lane == k, totals[k:k + 1], 0.0) for k in range(3))
    row_ref[...] = jnp.broadcast_to(row[None], row_ref.shape)
    copy.wait()


def halve_kernel(place_ref, keep_ref, got_ref, send_ref, rest_ref):
    mine = place_ref[1]
    send_ref[...] = keep_ref[1 - mine] + got_ref[1 - mine]
    rest_ref[...] = keep_ref[mine] + got_ref[mine]


def prepare_kernel(place_ref, texts_ref, unit_ref, factor_ref):
    first = pl.multiple_of((2 * place_ref[1] + place_ref[2]) * IMAGES, IMAGES)
    unit_ref[...], factor = normalized(texts_ref[pl.ds(first, IMAGES), :])
    factor_ref[...] = jnp.broadcast_to(factor, factor_ref.shape)


def text_end_kernel(temp_ref, unit_ref, factor_ref, rest_ref, got_ref, out_ref):
    scale = jnp.exp(jnp.full((1, WIDTH), temp_ref[0], F32))
    out_ref[...] = back_normal(unit_ref[...], factor_ref[:, :1], scale * (rest_ref[...] + got_ref[...]))


def join_kernel(own_ref, near_ref, far_ref, mine_ref, other_ref):
    mine_ref[...] = own_ref[...] + near_ref[:IMAGES, :] + far_ref[:IMAGES, :]
    other_ref[...] = near_ref[IMAGES:, :] + far_ref[IMAGES:, :]


def image_end_kernel(temp_ref, images_ref, mine_ref, got_ref, out_ref):
    unit, factor = normalized(images_ref[...])
    scale = jnp.exp(jnp.full((1, WIDTH), temp_ref[0], F32))
    out_ref[...] = back_normal(unit, factor, scale * (mine_ref[...] + got_ref[...]))


def again_kernel(row_ref, out_ref):
    total = jnp.sum(row_ref[...], axis=0, keepdims=True)
    out_ref[...] = jnp.broadcast_to(total, out_ref.shape)


def sums_end_kernel(temp_ref, row_ref, loss_ref, temp_grad_ref, bias_grad_ref):
    total = jnp.sum(row_ref[...], axis=0)
    lane = lax.broadcasted_iota(jnp.int32, (1, IMAGES), 1)
    scale = jnp.exp(jnp.full((1, IMAGES), temp_ref[0], F32))
    loss_ref[0] = jnp.sum(jnp.where(lane == 0, total, 0.0)) * (1.0 / BATCH)
    bias_grad_ref[0] = jnp.sum(jnp.where(lane == 1, total, 0.0))
    temp_grad_ref[0] = jnp.sum(jnp.where(lane == 2, total * scale, 0.0))


def per_device(images, texts, positive, temp_log, bias_arg):
    place = jnp.stack([lax.axis_index(BLK) * TEXTS, lax.axis_index("y_hi"), lax.axis_index("core")]).astype(jnp.int32)
    block_flops = 6 * TEXTS * IMAGES * WIDTH
    positive = positive.reshape(1, IMAGES)
    (mine,) = call(pack_kernel, [shape(IMAGES + PAD_ROWS, WIDTH, dtype=BF16)], images, positive)
    other = swapped(mine, "core")
    near = [to_side(mine, 1), to_side(other, 1)]
    text_unit, dx0, own_grads, sums = call(
        own_kernel,
        [shape(TEXTS, WIDTH, dtype=BF16), shape(IMAGES, WIDTH), shape(TEXTS, IMAGES, dtype=BF16), shape(8, IMAGES)],
        texts, mine, place, temp_log, bias_arg, flops=block_flops, smem_in=(2, 3, 4),
    )
    near[0], text_unit = lax.optimization_barrier((near[0], text_unit))
    far = [to_side(near[0], 1), to_side(near[1], 1)]
    staging = [pltpu.VMEM((PAIR, WIDTH), F32), pltpu.SemaphoreType.DMA(())]
    near_dx, dy, sums = call(
        near_kernel, [shape(PAIR, WIDTH), shape(TEXTS, WIDTH), shape(8, IMAGES)],
        text_unit, *near, place, temp_log, bias_arg, mine, own_grads, sums,
        flops=2 * block_flops, smem_in=(3, 4, 5), any_out=(0,), scratch=staging,
    )
    near_dx = to_side(near_dx, -1)
    far_dx, send, keep, row = call(
        far_kernel, [shape(PAIR, WIDTH)] + [shape(2, IMAGES, WIDTH)] * 2 + [shape(RING, 1, IMAGES)],
        text_unit, *far, place, temp_log, bias_arg, dy, sums,
        flops=2 * block_flops, smem_in=(3, 4, 5), any_out=(0,),
        scratch=staging + [pltpu.VMEM((TEXTS, WIDTH), F32)],
    )
    far_dx = to_side(far_dx, -2)
    got = swapped(send, "core")
    row = lax.all_to_all(row, "z", 0, 0, tiled=True)
    near_dx, got = lax.optimization_barrier((near_dx, got))
    send, rest = call(halve_kernel, [shape(IMAGES, WIDTH)] * 2, place, keep, got, smem_in=(0,))
    got = swapped(send, "y_hi")
    unit, factor = call(
        prepare_kernel, [shape(IMAGES, WIDTH), shape(IMAGES, IMAGES)], place, texts, smem_in=(0,)
    )
    row, unit = lax.optimization_barrier((row, unit))
    (row,) = call(again_kernel, [shape(RING, 1, IMAGES)], row, flops=5 * 10**9)
    row = lax.all_to_all(row, PLANE, 0, 0, tiled=True)
    mine, other = call(join_kernel, [shape(IMAGES, WIDTH)] * 2, dx0, near_dx, far_dx)
    other = swapped(other, "core")
    (text_grad,) = call(
        text_end_kernel, [shape(IMAGES, WIDTH)], temp_log, unit, factor, rest, got,
        smem_in=(0,), flops=8 * 10**9,
    )
    mine, text_grad = lax.optimization_barrier((mine, text_grad))
    (image_grad,) = call(
        image_end_kernel, [shape(IMAGES, WIDTH)], temp_log, images, mine, other, smem_in=(0,)
    )
    row, image_grad, text_grad = lax.optimization_barrier((row, image_grad, text_grad))
    loss, temp_grad, bias_grad = call(
        sums_end_kernel, [shape(1)] * 3, temp_log, row, smem_in=(0,), smem_out=(0, 1, 2)
    )
    return (loss, image_grad, text_grad, temp_grad, bias_grad)


def solution(mesh):
    axes = BLK + ("y_hi", "core")
    fine = Mesh(mesh.devices.reshape(SIZES), axes)
    placed = (P(axes, None), P(BLK, None), P(axes), P(), P())
    return jax.shard_map(
        per_device,
        mesh=fine,
        in_specs=placed,
        out_specs=(P(), P(axes, None), P(axes, None), P(), P()),
        check_vma=False,
    )
```

```python
import jax
import jax.numpy as jnp
from jax import lax
from jax.experimental import pallas as pl
from jax.experimental.pallas import tpu as pltpu
from jax.sharding import Mesh, PartitionSpec as P

EPS = 1e-06
BLK = ("y_lo", "z", "x")
PLANE = ("y_lo", "x", "y_hi", "core")
SIZES = (2, 32, 4, 2, 2)
WIDTH = 1152
IMAGES = 128
TEXTS = 512
PAD_ROWS = 16
PAIR = 2 * IMAGES
BATCH = 131072
RING = 32
F32 = jnp.float32
BF16 = jnp.bfloat16


def shape(*dims, dtype=F32):
    return jax.ShapeDtypeStruct(dims, dtype)


def call(body, outs, *args, flops=0, smem_in=(), smem_out=(), any_out=(), scratch=()):
    moved = sum(a.size * a.dtype.itemsize for a in args)
    moved += sum(o.size * o.dtype.itemsize for o in outs)
    scalar = pl.BlockSpec(memory_space=pltpu.SMEM)
    vector = pl.BlockSpec(memory_space=pltpu.VMEM)
    placed = pl.BlockSpec(memory_space=pl.ANY)
    return pl.pallas_call(
        body,
        out_shape=outs,
        in_specs=[scalar if k in smem_in else vector for k in range(len(args))],
        out_specs=[scalar if k in smem_out else placed if k in any_out else vector for k in range(len(outs))],
        scratch_shapes=list(scratch),
        compiler_params=pltpu.CompilerParams(vmem_limit_bytes=20 * 1024 * 1024),
        cost_estimate=pl.CostEstimate(flops=flops, bytes_accessed=moved, transcendentals=0),
    )(*args)


def to_side(value, by):
    count = lax.axis_size(BLK)
    pairs = []
    for shard in range(count):
        pairs.append((2 * shard, 2 * ((shard + by) % count)))
        pairs.append((2 * shard + 1, 2 * ((shard - by) % count) + 1))
    return lax.ppermute(value, BLK + ("core",), pairs)


def swapped(value, axis):
    return lax.ppermute(value, axis, [(0, 1), (1, 0)])


def normalized(values):
    full = values.astype(F32)
    factor = lax.rsqrt(jnp.sum(full * full, axis=-1, keepdims=True) + EPS)
    return full * factor, factor


def back_normal(unit_f, factor, dunit):
    return factor * (dunit - unit_f * jnp.sum(unit_f * dunit, axis=-1, keepdims=True))


def pack_kernel(images_ref, positive_ref, out_ref):
    unit, _ = normalized(images_ref[...])
    out_ref[:IMAGES, :] = unit.astype(BF16)
    pos = positive_ref[...]
    row = lax.broadcasted_iota(jnp.int32, (PAD_ROWS, IMAGES), 0)
    digit = jnp.where(row == 0, pos >> 12, jnp.where(row == 1, (pos >> 6) & 63, pos & 63))
    out_ref[IMAGES:, :] = jnp.zeros((PAD_ROWS, WIDTH), BF16)
    out_ref[IMAGES:, :IMAGES] = digit.astype(F32).astype(BF16)


def pair_block(packed_refs, text_unit, place_ref, temp_ref, bias_ref):
    count = len(packed_refs) * IMAGES
    unit = jnp.concatenate([ref[:IMAGES, :] for ref in packed_refs], axis=0)
    digits = jnp.concatenate([ref[IMAGES:, :IMAGES] for ref in packed_refs], axis=1).astype(F32).astype(jnp.int32)
    row = lax.broadcasted_iota(jnp.int32, (PAD_ROWS, count), 0)
    weight = jnp.where(row == 0, 4096, jnp.where(row == 1, 64, jnp.where(row == 2, 1, 0)))
    pos = jnp.sum(digits * weight, axis=0, keepdims=True) - place_ref[0]
    sim = lax.dot_general(text_unit, unit, (((1,), (1,)), ((), ())), preferred_element_type=F32)
    scale = jnp.exp(jnp.full((1, count), temp_ref[0], F32))
    logit = scale * sim + bias_ref[0]
    matching = lax.broadcasted_iota(jnp.int32, (TEXTS, count), 0) == pos
    against = jnp.where(matching, -logit, logit)
    small = jnp.exp(-jnp.abs(against))
    soft = jnp.maximum(against, 0.0) + jnp.log1p(small)
    sigmoid = jnp.where(against >= 0, 1.0, small) / (1.0 + small)
    grads = jnp.where(matching, -sigmoid, sigmoid)
    sums = [jnp.sum(v, axis=0, keepdims=True) for v in (soft, grads, grads * sim)]
    tile = jnp.concatenate(sums + [jnp.zeros((5, count), F32)], axis=0)
    for first in range(IMAGES, count, IMAGES):
        tile = tile[:, :IMAGES] + tile[:, first:first + IMAGES]
    return unit, grads.astype(BF16), tile


def image_part(grads, text_unit):
    return lax.dot_general(grads, text_unit, (((0,), (0,)), ((), ())), preferred_element_type=F32)


def text_part(grads, unit):
    return jnp.dot(grads, unit, preferred_element_type=F32)


def own_kernel(texts_ref, packed_ref, place_ref, temp_ref, bias_ref, text_ref, dx_ref, dy_ref, sums_ref):
    unit, _ = normalized(texts_ref[...])
    text_ref[...] = unit.astype(BF16)
    text_unit = text_ref[...]
    unit, grads, sums_ref[...] = pair_block([packed_ref], text_unit, place_ref, temp_ref, bias_ref)
    dx_ref[...] = image_part(grads, text_unit)
    dy_ref[...] = text_part(grads, unit)


def near_kernel(text_ref, first_ref, second_ref, place_ref, temp_ref, bias_ref, old_dy_ref, old_sums_ref,
                dx_ref, dy_ref, sums_ref, staged, sem):
    text_unit = text_ref[...]
    unit, grads, tile = pair_block([first_ref, second_ref], text_unit, place_ref, temp_ref, bias_ref)
    staged[...] = image_part(grads, text_unit)
    copy = pltpu.make_async_copy(staged, dx_ref, sem)
    copy.start()
    dy_ref[...] = old_dy_ref[...] + text_part(grads, unit)
    sums_ref[...] = old_sums_ref[...] + tile
    copy.wait()


def far_kernel(text_ref, first_ref, second_ref, place_ref, temp_ref, bias_ref, old_dy_ref, old_sums_ref,
               dx_ref, send_ref, keep_ref, row_ref, staged, sem, total):
    text_unit = text_ref[...]
    unit, grads, tile = pair_block([first_ref, second_ref], text_unit, place_ref, temp_ref, bias_ref)
    staged[...] = image_part(grads, text_unit)
    copy = pltpu.make_async_copy(staged, dx_ref, sem)
    copy.start()
    total[...] = old_dy_ref[...] + text_part(grads, unit)
    core = place_ref[2]
    for out_ref, owner in ((send_ref, 1 - core), (keep_ref, core)):
        for half in range(2):
            first = pl.multiple_of((2 * half + owner) * IMAGES, IMAGES)
            out_ref[half] = total[pl.ds(first, IMAGES), :]
    totals = jnp.sum(old_sums_ref[...] + tile, axis=1, keepdims=True)
    lane = lax.broadcasted_iota(jnp.int32, (1, IMAGES), 1)
    row = sum(jnp.where(lane == k, totals[k:k + 1], 0.0) for k in range(3))
    row_ref[...] = jnp.broadcast_to(row[None], row_ref.shape)
    copy.wait()


def halve_kernel(place_ref, keep_ref, got_ref, send_ref, rest_ref):
    mine = place_ref[1]
    send_ref[...] = keep_ref[1 - mine] + got_ref[1 - mine]
    rest_ref[...] = keep_ref[mine] + got_ref[mine]


def prepare_kernel(place_ref, texts_ref, unit_ref, factor_ref):
    first = pl.multiple_of((2 * place_ref[1] + place_ref[2]) * IMAGES, IMAGES)
    unit_ref[...], factor = normalized(texts_ref[pl.ds(first, IMAGES), :])
    factor_ref[...] = jnp.broadcast_to(factor, factor_ref.shape)


def text_end_kernel(temp_ref, unit_ref, factor_ref, rest_ref, got_ref, out_ref):
    scale = jnp.exp(jnp.full((1, WIDTH), temp_ref[0], F32))
    out_ref[...] = back_normal(unit_ref[...], factor_ref[:, :1], scale * (rest_ref[...] + got_ref[...]))


def join_kernel(own_ref, near_ref, far_ref, mine_ref, other_ref):
    mine_ref[...] = own_ref[...] + near_ref[:IMAGES, :] + far_ref[:IMAGES, :]
    other_ref[...] = near_ref[IMAGES:, :] + far_ref[IMAGES:, :]


def again_kernel(row_ref, out_ref):
    total = jnp.sum(row_ref[...], axis=0, keepdims=True)
    out_ref[...] = jnp.broadcast_to(total, out_ref.shape)


def end_kernel(temp_ref, images_ref, mine_ref, got_ref, row_ref, image_ref, loss_ref, temp_grad_ref, bias_grad_ref):
    total = jnp.sum(row_ref[...], axis=0)
    lane = lax.broadcasted_iota(jnp.int32, (1, IMAGES), 1)
    scale = jnp.exp(jnp.full((1, IMAGES), temp_ref[0], F32))
    loss_ref[0] = jnp.sum(jnp.where(lane == 0, total, 0.0)) * (1.0 / BATCH)
    bias_grad_ref[0] = jnp.sum(jnp.where(lane == 1, total, 0.0))
    temp_grad_ref[0] = jnp.sum(jnp.where(lane == 2, total * scale, 0.0))
    unit, factor = normalized(images_ref[...])
    scale = jnp.exp(jnp.full((1, WIDTH), temp_ref[0], F32))
    image_ref[...] = back_normal(unit, factor, scale * (mine_ref[...] + got_ref[...]))


def per_device(images, texts, positive, temp_log, bias_arg):
    place = jnp.stack([lax.axis_index(BLK) * TEXTS, lax.axis_index("y_hi"), lax.axis_index("core")]).astype(jnp.int32)
    block_flops = 6 * TEXTS * IMAGES * WIDTH
    positive = positive.reshape(1, IMAGES)
    (mine,) = call(pack_kernel, [shape(IMAGES + PAD_ROWS, WIDTH, dtype=BF16)], images, positive)
    other = swapped(mine, "core")
    near = [to_side(mine, 1), to_side(other, 1)]
    text_unit, dx0, dy, sums = call(
        own_kernel,
        [shape(TEXTS, WIDTH, dtype=BF16), shape(IMAGES, WIDTH), shape(TEXTS, WIDTH), shape(8, IMAGES)],
        texts, mine, place, temp_log, bias_arg, flops=block_flops, smem_in=(2, 3, 4),
    )
    near[0], text_unit = lax.optimization_barrier((near[0], text_unit))
    far = [to_side(near[0], 1), to_side(near[1], 1)]
    staging = [pltpu.VMEM((PAIR, WIDTH), F32), pltpu.SemaphoreType.DMA(())]
    near_dx, dy, sums = call(
        near_kernel, [shape(PAIR, WIDTH), shape(TEXTS, WIDTH), shape(8, IMAGES)],
        text_unit, *near, place, temp_log, bias_arg, dy, sums,
        flops=2 * block_flops, smem_in=(3, 4, 5), any_out=(0,), scratch=staging,
    )
    near_dx = to_side(near_dx, -1)
    far_dx, send, keep, row = call(
        far_kernel, [shape(PAIR, WIDTH)] + [shape(2, IMAGES, WIDTH)] * 2 + [shape(RING, 1, IMAGES)],
        text_unit, *far, place, temp_log, bias_arg, dy, sums,
        flops=2 * block_flops, smem_in=(3, 4, 5), any_out=(0,),
        scratch=staging + [pltpu.VMEM((TEXTS, WIDTH), F32)],
    )
    far_dx = to_side(far_dx, -2)
    got = swapped(send, "core")
    row = lax.all_to_all(row, "z", 0, 0, tiled=True)
    near_dx, got = lax.optimization_barrier((near_dx, got))
    send, rest = call(halve_kernel, [shape(IMAGES, WIDTH)] * 2, place, keep, got, smem_in=(0,))
    got = swapped(send, "y_hi")
    unit, factor = call(
        prepare_kernel, [shape(IMAGES, WIDTH), shape(IMAGES, IMAGES)], place, texts, smem_in=(0,)
    )
    row, unit = lax.optimization_barrier((row, unit))
    (row,) = call(again_kernel, [shape(RING, 1, IMAGES)], row, flops=5 * 10**9)
    row = lax.all_to_all(row, PLANE, 0, 0, tiled=True)
    mine, other = call(join_kernel, [shape(IMAGES, WIDTH)] * 2, dx0, near_dx, far_dx)
    other = swapped(other, "core")
    (text_grad,) = call(
        text_end_kernel, [shape(IMAGES, WIDTH)], temp_log, unit, factor, rest, got,
        smem_in=(0,), flops=8 * 10**9,
    )
    mine, text_grad = lax.optimization_barrier((mine, text_grad))
    image_grad, loss, temp_grad, bias_grad = call(
        end_kernel, [shape(IMAGES, WIDTH)] + [shape(1)] * 3, temp_log, images, mine, other, row,
        smem_in=(0,), smem_out=(1, 2, 3),
    )
    return (loss, image_grad, text_grad, temp_grad, bias_grad)


def solution(mesh):
    axes = BLK + ("y_hi", "core")
    fine = Mesh(mesh.devices.reshape(SIZES), axes)
    placed = (P(axes, None), P(BLK, None), P(axes), P(), P())
    return jax.shard_map(
        per_device,
        mesh=fine,
        in_specs=placed,
        out_specs=(P(), P(axes, None), P(axes, None), P(), P()),
        check_vma=False,
    )
```
